128 devices in a mesh: section: 2 (over core), seq: 16 (over z, y), tensor: 4 (over x).
Axes of the slice: x: 4, y: 4, z: 4, core: 2. Of those that a mesh axis runs over, the one named last changes fastest.
Arguments:
- vit_hidden: bfloat16 [2, 4096, 6400], P('section', 'seq', 'tensor'), may hold values from -6 to 6
- vit_resid: bfloat16 [2, 4096, 3200], P('section', 'seq', 'tensor'), may hold values from -6 to 6
- fc2_weight: bfloat16 [6400, 3200], P('tensor', 'seq'), may hold values from -0.078125 to 0.078125
- layer_scale: float32 [3200], P('tensor'), may hold values from 0.3 to 3
- norm_gain: float32 [12800], replicated, may hold values from 0.5 to 1.5
- norm_bias: float32 [12800], replicated, may hold values from -3 to 3
- proj_weight: bfloat16 [12800, 7168], P('seq', 'tensor'), may hold values from -4 to 4
- proj2_weight: bfloat16 [7168, 4, 1792], P('tensor', None, 'seq'), may hold values from -0.0625 to 0.0625
- proj2_bias: float32 [7168], P('tensor'), may hold values from -4 to 4
- text_embed: bfloat16 [2, 8192, 7168], P('section', 'seq', 'tensor'), may hold values from -120 to 120
- visual_slot: int32 [2, 64], P('section'), may hold values from 0 to 511, as said below
- rms_gain: float32 [7168], P('tensor'), may hold values from 0.5 to 2
- qkv_weight: bfloat16 [7168, 4608], P('tensor'), may hold values from -0.0625 to 0.0625
Outputs:
- qkv: bfloat16 [2, 8192, 4608], P('section', ('seq', 'tensor'))
The draws below stay inside these ranges and needn't reach their ends.
Inputs may be any that keep to these rules, and one draw needn't show every extreme that they name: `visual_slot`: each row lists 64 distinct sequence blocks of 16 rows, the place of each visual block, in no particular order; the first and the last block of the sequence always hold visual rows, and visual block 0 always goes to sequence block 256.
All inputs are finite; a program needn't handle non-finite values.
Results may differ from the reference program's by a relative error of at most 0.022.
Values may be sent and summed in bfloat16 or wider, within the bound.
No kernel may reach another device: no remote copies, remote signals or barrier semaphores. Data moves between devices by JAX's collectives and lax.ppermute only.
A program may use at most 128 MiB of HBM per device.

```python
import math
import jax
import jax.numpy as jnp
from jax import lax

DV = 3200
HV = 6400
D = 7168
G = 32
BLK = 16
QKV = 4608
PATCHES = 4096
SEQ = 8192
NB = 64
SB = 512
N_SEQ = 16
N_TENSOR = 4


def draw_proj_weight(key, part):
    key = jax.random.fold_in(key, 11)
    first_key = jax.random.fold_in(key, 0)
    column_scale = 10.0 ** (jnp.arange(D, dtype=jnp.float32) / D)
    sampled = jnp.clip(jax.random.normal(first_key, (4 * DV, D), jnp.float32), -4.0, 4.0)
    return (sampled * column_scale / math.sqrt(4 * DV)).astype(jnp.bfloat16)


def draw_text_embed(key, part):
    key = jax.random.fold_in(key, 23)
    first_key, second_key = jax.random.split(key)
    column_scale = 10.0 ** (jnp.arange(D, dtype=jnp.float32) / D)
    row_scale = jnp.exp(jax.random.uniform(second_key, (2, SEQ, 1), jnp.float32, 0.0, 2.3))
    sampled = jnp.clip(jax.random.normal(first_key, (2, SEQ, D), jnp.float32), -4.0, 4.0)
    return (0.3 * sampled * row_scale * column_scale).astype(jnp.bfloat16)


def draw_visual_slot(key, part):
    key = jax.random.fold_in(key, 37)
    slot_keys = jax.random.split(key, 4)

    def one_sequence(choose_key, order_key):
        priority = jax.random.permutation(choose_key, SB).astype(jnp.int32)
        positions = jnp.arange(SB, dtype=jnp.int32)
        priority = jnp.where(positions == SB // 2, -3, priority)
        priority = jnp.where(positions == 0, -2, priority)
        priority = jnp.where(positions == SB - 1, -1, priority)
        chosen = jnp.argsort(priority, stable=True)[:NB].astype(jnp.int32)
        middle = chosen[:1]
        others = jax.random.permutation(order_key, chosen[1:]).astype(jnp.int32)
        return jnp.concatenate([middle, others]).astype(jnp.int32)
    return jnp.stack([one_sequence(slot_keys[0], slot_keys[1]), one_sequence(slot_keys[2], slot_keys[3])])


def block_levels(own_key, extent, pieces, low, high):
    level, own = 1.0, jax.random.fold_in(own_key, 6)
    for position, blocks in pieces:
        heights = jnp.exp(jax.random.uniform(jax.random.fold_in(own, position), (blocks,), jnp.float32, low / len(pieces), high / len(pieces)))
        level = level * jnp.repeat(heights, extent[position] // blocks).reshape([-1 if axis == position else 1 for axis in range(len(extent))])
    return level


def noise(stream_key, dims, scale, bound, cuts=(), kind=jnp.bfloat16):
    array = jax.random.normal(stream_key, dims, jnp.float32) * scale
    if len(cuts) > 0:
        array = block_levels(stream_key, dims, cuts, -0.22, 0.18) * array
    return jnp.clip(array, min=-bound, max=bound).astype(kind)


def setup_inputs(seed: int = 0) -> dict:
    streams_of = jax.random.split(jax.random.key(seed), 14)
    return {
        "vit_hidden": noise(streams_of[0], (2, PATCHES, HV), 1.0, 6.0, ((0, 2), (1, 16), (2, 4))),
        "vit_resid": noise(streams_of[1], (2, PATCHES, DV), 1.0, 6.0, ((0, 2), (1, 16), (2, 4))),
        "fc2_weight": noise(streams_of[2], (HV, DV), HV ** -0.5, 0.078125, ((0, 4), (1, 16))),
        "layer_scale": jnp.clip(jnp.exp(math.log(3.0) - 2.3025851 * jax.random.uniform(streams_of[3], (DV,), jnp.float32) ** block_levels(streams_of[3], (DV,), ((0, 4),), -0.2, 0.2)), 0.3, 3.0),
        "norm_gain": jnp.clip(1.0 + 0.1 * jax.random.normal(streams_of[4], (4 * DV,), jnp.float32), 0.5, 1.5),
        "norm_bias": noise(streams_of[5], (4 * DV,), 0.5, 3.0, (), jnp.float32),
        "proj_weight": draw_proj_weight(jax.random.fold_in(streams_of[13], 71), 0),
        "proj2_weight": noise(streams_of[7], (D, N_TENSOR, D // N_TENSOR), D ** -0.5, 0.0625, ((0, 4), (2, 16))),
        "proj2_bias": noise(streams_of[8], (D,), 1.0, 4.0, ((0, 4),), jnp.float32),
        "text_embed": draw_text_embed(jax.random.fold_in(streams_of[13], 71), 0),
        "visual_slot": draw_visual_slot(jax.random.fold_in(streams_of[13], 71), 0),
        "rms_gain": jnp.clip(jnp.exp(math.log(2.0) - 1.3862944 * jax.random.uniform(streams_of[11], (D,), jnp.float32) ** block_levels(streams_of[11], (D,), ((0, 4),), -0.2, 0.2)), 0.5, 2.0),
        "qkv_weight": noise(streams_of[12], (D, QKV), D ** -0.5, 0.0625, ((0, 4),)),
    }


norm_eps = 1e-05

def shuffle_tokens(layer_out, grid_cols):
    patch_total, width_in = layer_out.shape
    row_count = patch_total // grid_cols
    patch_grid = layer_out.reshape(row_count // 2, 2, grid_cols // 2, 2, width_in)
    return patch_grid.transpose(0, 2, 1, 3, 4).reshape(row_count // 2 * (grid_cols // 2), 4 * width_in)

def layer_norm_rows(values, gain, bias):
    widened = values.astype(jnp.float32)
    center = lax.optimization_barrier(jnp.mean(widened, axis=-1, keepdims=True))
    spread = lax.optimization_barrier(jnp.mean(jnp.square(widened - center), axis=-1, keepdims=True))
    return ((widened - center) * lax.rsqrt(spread + norm_eps) * gain + bias).astype(jnp.bfloat16)

def projector_sum(proj_in, proj_weight):
    block_width = proj_in.shape[1] // N_SEQ

    def accumulate(running, block_index):
        begin = (block_index * block_width).astype(jnp.int32)
        inputs_part = lax.dynamic_slice_in_dim(proj_in, begin, block_width, 1)
        weight_part = lax.dynamic_slice_in_dim(proj_weight, begin, block_width, 0)
        product = jnp.dot(inputs_part, weight_part, preferred_element_type=jnp.float32)
        rounded = lax.optimization_barrier(product.astype(jnp.bfloat16)).astype(jnp.float32)
        return (running + rounded, None)
    initial = jnp.zeros((proj_in.shape[0], proj_weight.shape[1]), jnp.float32)
    running, _ = lax.scan(accumulate, initial, jnp.arange(N_SEQ, dtype=jnp.int32))
    return running

def qkv_sum(normed, qkv_weight):
    block_width = normed.shape[1] // N_TENSOR
    running = jnp.zeros((normed.shape[0], qkv_weight.shape[1]), jnp.float32)
    for tensor_block in range(N_TENSOR):
        lower = tensor_block * block_width
        product = jnp.dot(normed[:, lower:lower + block_width], qkv_weight[lower:lower + block_width], preferred_element_type=jnp.float32)
        running = running + lax.optimization_barrier(product.astype(jnp.bfloat16)).astype(jnp.float32)
    return running.astype(jnp.bfloat16)

def reference(vit_hidden, vit_resid, fc2_weight, layer_scale, norm_gain, norm_bias, proj_weight, proj2_weight, proj2_bias, text_embed, visual_slot, rms_gain, qkv_weight):
    second_map = proj2_weight.reshape(proj2_weight.shape[0], -1)
    results = []
    for section_slot in range(2):
        source_slot = 1 - section_slot
        mlp = jnp.dot(vit_hidden[source_slot], fc2_weight, preferred_element_type=jnp.float32)
        layer_out = (vit_resid[source_slot].astype(jnp.float32) + layer_scale * mlp).astype(jnp.bfloat16)
        proj_in = layer_norm_rows(shuffle_tokens(layer_out, G), norm_gain, norm_bias)
        projected = projector_sum(proj_in, proj_weight)
        proj_hidden = jax.nn.gelu(projected, approximate=False).astype(jnp.bfloat16)
        visual = (jnp.dot(proj_hidden, second_map, preferred_element_type=jnp.float32) + proj2_bias).astype(jnp.bfloat16)
        row_index = (visual_slot[section_slot][:, None] * BLK + jnp.arange(BLK, dtype=jnp.int32)[None, :]).reshape(-1).astype(jnp.int32)
        merged = text_embed[section_slot].at[row_index].set(visual)
        widened = merged.astype(jnp.float32)
        mean_square = lax.optimization_barrier(jnp.mean(widened * widened, axis=1, keepdims=True))
        normed = (widened * lax.rsqrt(mean_square + norm_eps) * rms_gain).astype(jnp.bfloat16)
        results.append(qkv_sum(normed, qkv_weight))
    return jnp.stack(results)
```

```python
import jax
import jax.numpy as jnp
import numpy as np
from jax import lax
from jax.experimental import pallas as pl
from jax.experimental.pallas import tpu as pltpu
from jax.sharding import PartitionSpec as P

D = 7168
G = 32
BLK = 16
RING = 4

norm_eps = 1e-05
bf16 = jnp.bfloat16
f32 = jnp.float32
ALL = ("section", "seq", "tensor")


def move(block, target):
    route = []
    for c in range(2):
        for z in range(RING):
            for y in range(RING):
                for x in range(RING):
                    tc, tz, ty, tx = target(c, z, y, x)
                    here = ((c * RING + z) * RING + y) * RING + x
                    there = ((tc % 2 * RING + tz % RING) * RING + ty % RING) * RING + tx % RING
                    route.append((here, there))
    return lax.ppermute(block, ALL, route)


def along(block, axis, hop):
    axes = axis * 2 if len(axis) == 1 else axis

    def target(c, z, y, x):
        return (c, z + hop * (axes[c] == "z"), y + hop * (axes[c] == "y"), x + hop * (axes[c] == "x"))

    return move(block, target)


def pick(array, index, axis):
    return lax.dynamic_index_in_dim(array, index % RING, axis, keepdims=False)


def put(target, block, index, axis):
    return lax.dynamic_update_index_in_dim(target, block, index % RING, axis)


HOPS = (2, 1, -1)


def gather_ring(block, axis, me, stack_axis=0):
    return stack_ring([(hop, along(block, axis, hop)) for hop in HOPS] + [(0, block)], me, stack_axis)


def stack_ring(parts, me, stack_axis=0):
    shape = parts[0][1].shape
    stacked = jnp.zeros(shape[:stack_axis] + (RING,) + shape[stack_axis:], parts[0][1].dtype)
    for hop, part in parts:
        stacked = put(stacked, part, me - hop, stack_axis)
    return stacked


def sum_ring(term, axis, wire=bf16):
    arrived = [along(term(hop).astype(wire), axis, hop) for hop in HOPS]
    total = term(0)
    for part in arrived:
        total = total + part.astype(f32)
    return total


def order_ring(parts, me):
    blocks = [parts[hop] for hop in (0, 1, 2, -1)]
    return [lax.select_n((me - owner) % RING, *blocks) for owner in range(RING)]


def swap_ring(blocks, axis, me):
    parts = {hop: along(pick(blocks, me + hop, 0), axis, hop) for hop in HOPS}
    parts[0] = pick(blocks, me, 0)
    return order_ring(parts, me)


def pick_groups(groups, me):
    return jnp.stack([pick(groups, me + hop, 0) for hop in range(RING)])


def in_parts(value):
    high = lax.reduce_precision(value, 8, 7)
    middle = lax.reduce_precision(value - high, 8, 7)
    return [high, middle, lax.reduce_precision(value - high - middle, 8, 7)]


def after(value, *others):
    return lax.optimization_barrier((value, others))[0]


VMEM = 40 * 2**20


def to_ring(step):
    return RING - 1 - step


def seen_kernel(x_ref, visual_ref, gain_ref, extra_ref, weight_ref, *outs):
    seen = visual_ref[...].astype(f32)
    squares = jnp.sum(seen * seen, axis=1, keepdims=True)
    high = squares.astype(bf16).astype(f32)
    middle = (squares - high).astype(bf16).astype(f32)
    lane = lax.broadcasted_iota(jnp.int32, extra_ref.shape[1:], 1)
    extra = extra_ref[0]
    for place, part in enumerate((high, middle, squares - high - middle)):
        extra = jnp.where(lane == place, part, extra)
    total = dot((seen * gain_ref[...]).astype(bf16), weight_ref[...])
    columns = total.shape[1]

    def write(step):
        @pl.when(pl.program_id(0) == step)
        def _():
            outs[step][:, :columns] = total.astype(outs[step].dtype)
            outs[step][:, columns:] = extra.astype(outs[step].dtype)

    for step in range(RING):
        write(step)


def seen_terms(x, visual, gain, extra, weight):
    rows, width = visual.shape
    columns = weight.shape[1] // RING
    lanes = extra.shape[2]
    return pl.pallas_call(
        seen_kernel,
        grid_spec=pltpu.PrefetchScalarGridSpec(
            num_scalar_prefetch=1,
            grid=(RING,),
            in_specs=[
                pl.BlockSpec((rows, width), lambda i, x: (0, 0)),
                pl.BlockSpec((1, width), lambda i, x: (0, 0)),
                pl.BlockSpec((1, rows, lanes), lambda i, x: ((x[0] + to_ring(i)) % RING, 0, 0)),
                pl.BlockSpec((width, columns), lambda i, x: (0, (x[0] + to_ring(i)) % RING)),
            ],
            out_specs=[pl.BlockSpec((rows, columns + lanes), lambda i, x: (0, 0))] * RING,
        ),
        out_shape=[jax.ShapeDtypeStruct((rows, columns + lanes), kind) for kind in (bf16, bf16, bf16, f32)],
        compiler_params=pltpu.CompilerParams(vmem_limit_bytes=VMEM),
        cost_estimate=pl.CostEstimate(
            flops=2 * rows * width * columns * RING, bytes_accessed=2 * RING * width * columns, transcendentals=0
        ),
    )(x.reshape(1), visual, gain.reshape(1, width), extra, weight)


def choose_kernel(array_ref, place_ref, *refs):
    arrays, chosen = refs[:RING], refs[RING:]
    for to, out in enumerate(chosen):
        for i in range(out.shape[0]):
            which, place = array_ref[to * out.shape[0] + i], place_ref[to * out.shape[0] + i]
            block = arrays[0][place]
            for other in range(1, RING):
                block = jnp.where(which == other, arrays[other][place], block)
            out[i] = block


def choose_blocks(array, place, arrays):
    count = array.shape[0] // RING
    shape = jax.ShapeDtypeStruct((count,) + arrays[0].shape[1:], arrays[0].dtype)
    return pl.pallas_call(
        choose_kernel,
        in_specs=[pl.BlockSpec(memory_space=pltpu.SMEM)] * 2 + [pl.BlockSpec(memory_space=pltpu.VMEM)] * RING,
        out_specs=[pl.BlockSpec(memory_space=pltpu.VMEM)] * RING,
        out_shape=[shape] * RING,
        compiler_params=pltpu.CompilerParams(vmem_limit_bytes=VMEM),
        cost_estimate=pl.CostEstimate(flops=0, bytes_accessed=2 * RING * arrays[0].size, transcendentals=0),
    )(array, place, *arrays)


def dot(a, b):
    return jnp.dot(a, b, preferred_element_type=f32)


def dot_rows(a, b):
    return lax.dot_general(a, b, (((a.ndim - 1,), (1,)), ((), ())), preferred_element_type=f32)


def patch_order():
    order = np.arange(8 * G).reshape(4, 2, G // 2, 2).transpose(1, 3, 0, 2).reshape(-1)
    return np.eye(8 * G, dtype=np.float32)[order]


def local(
    vit_hidden,
    vit_resid,
    fc2_weight,
    layer_scale,
    norm_gain,
    norm_bias,
    proj_weight,
    proj2_weight,
    proj2_bias,
    text_embed,
    visual_slot,
    rms_gain,
    qkv_weight,
):
    c = lax.axis_index("section")
    s = lax.axis_index("seq")
    x = lax.axis_index("tensor")
    z, y = s // RING, s % RING
    order = jnp.asarray(patch_order(), bf16)
    tokens = vit_hidden.shape[1] // 4
    feats = layer_scale.shape[0]

    hidden = dot(vit_hidden[0].T, order.T).astype(bf16)
    behind = move(hidden, lambda c, z, y, x: (1 - c, z + 1, y, x))
    ahead = move(hidden, lambda c, z, y, x: (1 - c, z - 1, y, x))
    weight = fc2_weight.T
    weight_near = move(weight, lambda c, z, y, x: (c, z, y + 1 - 2 * c, x))
    own = move(hidden, lambda c, z, y, x: (1 - c, z, y, x))
    resid = dot(vit_resid[0].T, order.T).astype(bf16)
    resid = move(resid, lambda c, z, y, x: (1 - c, z, y, x - z))
    far = move(jnp.where(c == 0, behind, ahead), lambda c, z, y, x: (c, z + 1 - 2 * c, y, x))
    weight_far = move(weight_near, lambda c, z, y, x: (c, z, y + 1 - 2 * c, x))
    weight_other = move(weight_near, lambda c, z, y, x: (1 - c, z, y, x))
    resid = move(resid, lambda c, z, y, x: (c, z + x, y, x))
    weight_quarter = jnp.concatenate([weight, weight_near, weight_far, weight_other], axis=0)
    weight_quarter, resid = lax.optimization_barrier((weight_quarter, resid))

    second_half = proj2_weight.shape[1] // 2
    second_own = lax.dynamic_slice_in_dim(proj2_weight.transpose(1, 2, 0), c * second_half, second_half, 0)
    rings = [[RING * i + j for j in range(RING)] for i in range(RING)]
    second_own = lax.all_gather(second_own, "seq", axis=1, axis_index_groups=rings)

    resid = move(resid, lambda c, z, y, x: (c, z, y, x - z))
    scale = move(layer_scale, lambda c, z, y, x: (c, x, y, z))[:, None]

    terms = [dot(weight_quarter, rows) for rows in (own, ahead, far, behind)]
    mlp = sum_ring(lambda hop: lax.select_n((-x - hop - z) % RING, *terms), "x")
    mlp = mlp.reshape(RING, -1, 4 * tokens)
    mlp = [lax.select_n(jnp.where(c == 0, y - piece, piece - y) % RING, *mlp) for piece in range(RING)]
    layer_out = resid.astype(f32) + scale * jnp.concatenate(mlp, axis=0)
    layer_out = layer_out.astype(bf16).T.reshape(4, tokens, feats)
    widened = layer_out.astype(f32)
    part_mean = jnp.mean(widened, axis=(0, 2))
    part_dev = jnp.sum(jnp.square(widened - part_mean[:, None]), axis=(0, 2))
    part = jnp.stack([part_mean, part_dev])
    parts = jnp.stack([part] + [along(part, "z", hop) for hop in HOPS])
    mean = jnp.mean(parts[:, 0], axis=0)
    dev = jnp.sum(parts[:, 1], axis=0) + 4 * feats * jnp.sum(jnp.square(parts[:, 0] - mean), axis=0)
    inv = lax.rsqrt(dev / (4 * RING * feats) + norm_eps)
    gain = pick(norm_gain.reshape(4, RING, 1, feats), z, 1)
    bias = pick(norm_bias.reshape(4, RING, 1, feats), z, 1)
    proj_in = ((widened - mean[:, None]) * inv[:, None] * gain + bias).astype(bf16)
    proj_in = jnp.stack(swap_ring(proj_in, "z", z))
    proj_in = jnp.stack(swap_ring(proj_in, "y", y))
    text = after(text_embed[0], proj_in).astype(f32)
    arrived = [(hop, along(proj_in, "x", hop)) for hop in HOPS] + [(0, proj_in)]
    proj_in = stack_ring([(-hop, part) for hop, part in arrived], -x)
    text_terms = dot((text * rms_gain).astype(bf16), qkv_weight).astype(bf16)
    text_sum = lax.psum_scatter(text_terms, "tensor", scatter_dimension=0, tiled=True)
    second_other = move(second_own, lambda c, z, y, x: (1 - c, z, y, x))
    second_map = lax.dynamic_update_index_in_dim(jnp.zeros((2,) + second_own.shape, bf16), second_own, c, 0)
    second_map = lax.dynamic_update_index_in_dim(second_map, second_other, 1 - c, 0)
    second_map = second_map.reshape(RING, -1, proj2_weight.shape[0])
    text_parts = in_parts(jnp.sum(text * text, axis=1).reshape(RING, tokens, -1))
    text_parts = jnp.pad(jnp.concatenate(text_parts, axis=2), ((0, 0), (0, 0), (3, 125 - 3 * text_parts[0].shape[2])))
    proj_in, second_map, text_terms, text_parts = lax.optimization_barrier((proj_in, second_map, text_terms, text_parts))

    width = proj_weight.shape[1]
    half = width // 2

    def first_y(hop):
        return dot(pick(proj_in, y + hop, 1).reshape(RING * tokens, feats), proj_weight[:, :half])

    def first_z(hop):
        return dot(pick(proj_in, z + hop, 0).reshape(RING * tokens, feats), proj_weight[:, half:])

    over_y = sum_ring(first_y, "y").reshape(RING, tokens, half)
    over_z = sum_ring(first_z, "z").reshape(RING, tokens, half)
    left = sum_ring(lambda hop: pick(over_y, z + hop, 0), "z")
    right = sum_ring(lambda hop: pick(over_z, y + hop, 0), "y")
    proj_sum = jnp.concatenate([left, right], axis=1)
    proj_hidden = jax.nn.gelu(proj_sum, approximate=False).astype(bf16)

    hidden_ring = gather_ring(proj_hidden, "z", z).reshape(RING * tokens, width)
    second = sum_ring(lambda hop: dot_rows(hidden_ring, pick(second_map, x + hop, 0)), "x")
    piece = second.shape[1]
    bias_piece = lax.dynamic_slice_in_dim(proj2_bias, z * piece, piece)
    second = (second + bias_piece).astype(bf16).reshape(RING, tokens, piece)
    visual = jnp.concatenate(swap_ring(second, "z", z), axis=1)

    first, second = jnp.where(c == 0, y, z), jnp.where(c == 0, z, y)
    columns = qkv_weight.shape[1] // RING
    *sent, seen_sum = seen_terms(x, visual, rms_gain, text_parts, qkv_weight)
    for step in range(RING - 1):
        seen_sum = seen_sum + along(sent[step], "x", to_ring(step)).astype(f32)
    seen_squares = jnp.sum(seen_sum[:, columns : columns + 3], axis=1, keepdims=True)
    text_squares = seen_sum[:, columns + 3 : columns + 9].reshape(tokens, 3, -1).sum(axis=1).reshape(-1, 1)
    seen_qkv = (seen_sum[:, :columns] * lax.rsqrt(seen_squares / D + norm_eps)).astype(bf16)
    seen_ring = jnp.concatenate([seen_qkv] + [along(seen_qkv, "zy", hop) for hop in HOPS], axis=0)
    seen_all = [seen_ring] + [along(seen_ring, "yz", hop) for hop in HOPS]
    seen_all = [part.reshape(-1, BLK, columns) for part in seen_all]

    slots = visual_slot[0]
    local_blocks = text_embed.shape[1] // BLK
    wanted = s * local_blocks + jnp.arange(local_blocks, dtype=jnp.int32)
    matches = slots[None, :] == wanted[:, None]
    owned = jnp.any(matches, axis=1).reshape(RING, -1)
    source = jnp.sum(jnp.where(matches, jnp.arange(slots.shape[0], dtype=jnp.int32)[None, :], 0), axis=1).reshape(RING, -1)
    rows_out = text_embed.shape[1] // RING

    source = pick_groups(source, x).reshape(-1)
    shard_z, shard_y = source // (4 * RING), source // 4 % RING
    order_of = jnp.asarray([0, 2, 1, 3], jnp.int32)
    first_hop = order_of[(second - jnp.where(c == 0, shard_z, shard_y)) % RING]
    second_hop = order_of[(first - jnp.where(c == 0, shard_y, shard_z)) % RING]
    chosen = choose_blocks(second_hop, first_hop * 4 + source % 4, seen_all)
    parts = {0: chosen[0].reshape(rows_out, columns)}
    for hop in HOPS:
        parts[hop] = along(chosen[hop % RING].reshape(rows_out, columns), "x", hop)
    rows_seen = jnp.concatenate(order_ring(parts, x), axis=1)
    text_qkv = (text_sum.astype(f32) * lax.rsqrt(text_squares / D + norm_eps)).astype(bf16)
    row_owned = jnp.repeat(pick(owned, x, 0), BLK)
    return jnp.where(row_owned[:, None], rows_seen, text_qkv)[None]


def solution(mesh):
    return jax.shard_map(
        local,
        mesh=mesh,
        in_specs=(
            P("section", "seq", "tensor"),
            P("section", "seq", "tensor"),
            P("tensor", "seq"),
            P("tensor"),
            P(),
            P(),
            P("seq", "tensor"),
            P("tensor", None, "seq"),
            P("tensor"),
            P("section", "seq", "tensor"),
            P("section", None),
            P("tensor"),
            P("tensor", None),
        ),
        out_specs=P("section", ("seq", "tensor"), None),
        check_vma=False,
    )
```

```python
import jax
import jax.numpy as jnp
import numpy as np
from jax import lax
from jax.experimental import pallas as pl
from jax.experimental.pallas import tpu as pltpu
from jax.sharding import PartitionSpec as P

D = 7168
G = 32
BLK = 16
RING = 4

norm_eps = 1e-05
bf16 = jnp.bfloat16
f32 = jnp.float32
ALL = ("section", "seq", "tensor")


def move(block, target):
    route = []
    for c in range(2):
        for z in range(RING):
            for y in range(RING):
                for x in range(RING):
                    tc, tz, ty, tx = target(c, z, y, x)
                    here = ((c * RING + z) * RING + y) * RING + x
                    there = ((tc % 2 * RING + tz % RING) * RING + ty % RING) * RING + tx % RING
                    route.append((here, there))
    return lax.ppermute(block, ALL, route)


def along(block, axis, hop):
    axes = axis * 2 if len(axis) == 1 else axis

    def target(c, z, y, x):
        return (c, z + hop * (axes[c] == "z"), y + hop * (axes[c] == "y"), x + hop * (axes[c] == "x"))

    return move(block, target)


def pick(array, index, axis):
    return lax.dynamic_index_in_dim(array, index % RING, axis, keepdims=False)


def put(target, block, index, axis):
    return lax.dynamic_update_index_in_dim(target, block, index % RING, axis)


HOPS = (2, 1, -1)


def gather_ring(block, axis, me, stack_axis=0):
    return stack_ring([(hop, along(block, axis, hop)) for hop in HOPS] + [(0, block)], me, stack_axis)


def stack_ring(parts, me, stack_axis=0):
    shape = parts[0][1].shape
    stacked = jnp.zeros(shape[:stack_axis] + (RING,) + shape[stack_axis:], parts[0][1].dtype)
    for hop, part in parts:
        stacked = put(stacked, part, me - hop, stack_axis)
    return stacked


def sum_ring(term, axis, wire=bf16):
    arrived = [along(term(hop).astype(wire), axis, hop) for hop in HOPS]
    total = term(0)
    for part in arrived:
        total = total + part.astype(f32)
    return total


def order_ring(parts, me):
    blocks = [parts[hop] for hop in (0, 1, 2, -1)]
    return [lax.select_n((me - owner) % RING, *blocks) for owner in range(RING)]


def swap_ring(blocks, axis, me):
    parts = {hop: along(pick(blocks, me + hop, 0), axis, hop) for hop in HOPS}
    parts[0] = pick(blocks, me, 0)
    return order_ring(parts, me)


def pick_groups(groups, me):
    return jnp.stack([pick(groups, me + hop, 0) for hop in range(RING)])


def in_parts(value):
    high = lax.reduce_precision(value, 8, 7)
    middle = lax.reduce_precision(value - high, 8, 7)
    return [high, middle, lax.reduce_precision(value - high - middle, 8, 7)]


def after(value, *others):
    return lax.optimization_barrier((value, others))[0]


VMEM = 40 * 2**20


def to_ring(step):
    return RING - 1 - step


def seen_kernel(x_ref, visual_ref, gain_ref, extra_ref, weight_ref, *outs):
    seen = visual_ref[...].astype(f32)
    squares = jnp.sum(seen * seen, axis=1, keepdims=True)
    high = squares.astype(bf16).astype(f32)
    middle = (squares - high).astype(bf16).astype(f32)
    lane = lax.broadcasted_iota(jnp.int32, extra_ref.shape[1:], 1)
    extra = extra_ref[0]
    for place, part in enumerate((high, middle, squares - high - middle)):
        extra = jnp.where(lane == place, part, extra)
    total = dot((seen * gain_ref[...]).astype(bf16), weight_ref[...])
    columns = total.shape[1]

    def write(step):
        @pl.when(pl.program_id(0) == step)
        def _():
            outs[step][:, :columns] = total.astype(outs[step].dtype)
            outs[step][:, columns:] = extra.astype(outs[step].dtype)

    for step in range(RING):
        write(step)


def seen_terms(x, visual, gain, extra, weight):
    rows, width = visual.shape
    columns = weight.shape[1] // RING
    lanes = extra.shape[2]
    return pl.pallas_call(
        seen_kernel,
        grid_spec=pltpu.PrefetchScalarGridSpec(
            num_scalar_prefetch=1,
            grid=(RING,),
            in_specs=[
                pl.BlockSpec((rows, width), lambda i, x: (0, 0)),
                pl.BlockSpec((1, width), lambda i, x: (0, 0)),
                pl.BlockSpec((1, rows, lanes), lambda i, x: ((x[0] + to_ring(i)) % RING, 0, 0)),
                pl.BlockSpec((width, columns), lambda i, x: (0, (x[0] + to_ring(i)) % RING)),
            ],
            out_specs=[pl.BlockSpec((rows, columns + lanes), lambda i, x: (0, 0))] * RING,
        ),
        out_shape=[jax.ShapeDtypeStruct((rows, columns + lanes), kind) for kind in (bf16, bf16, bf16, f32)],
        compiler_params=pltpu.CompilerParams(vmem_limit_bytes=VMEM),
        cost_estimate=pl.CostEstimate(
            flops=2 * rows * width * columns * RING, bytes_accessed=2 * RING * width * columns, transcendentals=0
        ),
    )(x.reshape(1), visual, gain.reshape(1, width), extra, weight)


def choose_kernel(array_ref, place_ref, *refs):
    arrays, chosen = refs[:RING], refs[RING:]
    for to, out in enumerate(chosen):
        for i in range(out.shape[0]):
            which, place = array_ref[to * out.shape[0] + i], place_ref[to * out.shape[0] + i]
            block = arrays[0][place]
            for other in range(1, RING):
                block = jnp.where(which == other, arrays[other][place], block)
            out[i] = block


def choose_blocks(array, place, arrays):
    count = array.shape[0] // RING
    shape = jax.ShapeDtypeStruct((count,) + arrays[0].shape[1:], arrays[0].dtype)
    return pl.pallas_call(
        choose_kernel,
        in_specs=[pl.BlockSpec(memory_space=pltpu.SMEM)] * 2 + [pl.BlockSpec(memory_space=pltpu.VMEM)] * RING,
        out_specs=[pl.BlockSpec(memory_space=pltpu.VMEM)] * RING,
        out_shape=[shape] * RING,
        compiler_params=pltpu.CompilerParams(vmem_limit_bytes=VMEM),
        cost_estimate=pl.CostEstimate(flops=0, bytes_accessed=2 * RING * arrays[0].size, transcendentals=0),
    )(array, place, *arrays)


def dot(a, b):
    return jnp.dot(a, b, preferred_element_type=f32)


def dot_rows(a, b):
    return lax.dot_general(a, b, (((a.ndim - 1,), (1,)), ((), ())), preferred_element_type=f32)


def patch_order():
    order = np.arange(8 * G).reshape(4, 2, G // 2, 2).transpose(1, 3, 0, 2).reshape(-1)
    return np.eye(8 * G, dtype=np.float32)[order]


def local(
    vit_hidden,
    vit_resid,
    fc2_weight,
    layer_scale,
    norm_gain,
    norm_bias,
    proj_weight,
    proj2_weight,
    proj2_bias,
    text_embed,
    visual_slot,
    rms_gain,
    qkv_weight,
):
    c = lax.axis_index("section")
    s = lax.axis_index("seq")
    x = lax.axis_index("tensor")
    z, y = s // RING, s % RING
    order = jnp.asarray(patch_order(), bf16)
    tokens = vit_hidden.shape[1] // 4
    feats = layer_scale.shape[0]

    hidden = dot(vit_hidden[0].T, order.T).astype(bf16)
    behind = move(hidden, lambda c, z, y, x: (1 - c, z + 1, y, x))
    ahead = move(hidden, lambda c, z, y, x: (1 - c, z - 1, y, x))
    weight = fc2_weight.T
    weight_near = move(weight, lambda c, z, y, x: (c, z, y + 1 - 2 * c, x))
    own = move(hidden, lambda c, z, y, x: (1 - c, z, y, x))
    resid = dot(vit_resid[0].T, order.T).astype(bf16)
    resid = move(resid, lambda c, z, y, x: (1 - c, z, y, x - z))
    far = move(jnp.where(c == 0, behind, ahead), lambda c, z, y, x: (c, z + 1 - 2 * c, y, x))
    weight_far = move(weight_near, lambda c, z, y, x: (c, z, y + 1 - 2 * c, x))
    weight_other = move(weight_near, lambda c, z, y, x: (1 - c, z, y, x))
    resid = move(resid, lambda c, z, y, x: (c, z + x, y, x))
    weight_quarter = jnp.concatenate([weight, weight_near, weight_far, weight_other], axis=0)

    halves = proj2_weight.shape[1] // 2
    second_map = lax.dynamic_slice_in_dim(proj2_weight.transpose(1, 2, 0), c * halves, halves, 0)
    rings = [[16 * core + RING * i + j for core in range(2) for j in range(RING)] for i in range(RING)]
    second_map = lax.all_gather(second_map, ("section", "seq"), axis=0, axis_index_groups=rings)
    second_map = second_map.reshape((2, RING) + second_map.shape[1:])

    resid = move(resid, lambda c, z, y, x: (c, z, y, x - z))
    scale = move(layer_scale, lambda c, z, y, x: (c, x, y, z))[:, None]

    terms = [dot(weight_quarter, rows) for rows in (own, ahead, far, behind)]
    terms, resid = lax.optimization_barrier((terms, resid))
    mlp = sum_ring(lambda hop: lax.select_n((-x - hop - z) % RING, *terms), "x")
    mlp = mlp.reshape(RING, -1, 4 * tokens)
    mlp = [lax.select_n(jnp.where(c == 0, y - piece, piece - y) % RING, *mlp) for piece in range(RING)]
    layer_out = resid.astype(f32) + scale * jnp.concatenate(mlp, axis=0)
    layer_out = layer_out.astype(bf16).T.reshape(4, tokens, feats)
    widened = layer_out.astype(f32)
    part_mean = jnp.mean(widened, axis=(0, 2))
    part_dev = jnp.sum(jnp.square(widened - part_mean[:, None]), axis=(0, 2))
    part = jnp.stack([part_mean, part_dev])
    parts = jnp.stack([part] + [along(part, "z", hop) for hop in HOPS])
    mean = jnp.mean(parts[:, 0], axis=0)
    dev = jnp.sum(parts[:, 1], axis=0) + 4 * feats * jnp.sum(jnp.square(parts[:, 0] - mean), axis=0)
    inv = lax.rsqrt(dev / (4 * RING * feats) + norm_eps)
    gain = pick(norm_gain.reshape(4, RING, 1, feats), z, 1)
    bias = pick(norm_bias.reshape(4, RING, 1, feats), z, 1)
    proj_in = ((widened - mean[:, None]) * inv[:, None] * gain + bias).astype(bf16)
    proj_in = jnp.stack(swap_ring(proj_in, "z", z))
    proj_in = jnp.stack(swap_ring(proj_in, "y", y))
    text = after(text_embed[0], proj_in).astype(f32)
    arrived = [(hop, along(proj_in, "x", hop)) for hop in HOPS] + [(0, proj_in)]
    proj_in = stack_ring([(-hop, part) for hop, part in arrived], -x)
    text_terms = dot((text * rms_gain).astype(bf16), qkv_weight).astype(bf16)
    text_sum = lax.psum_scatter(text_terms, "tensor", scatter_dimension=0, tiled=True)
    text_parts = in_parts(jnp.sum(text * text, axis=1).reshape(RING, tokens, -1))
    text_parts = jnp.pad(jnp.concatenate(text_parts, axis=2), ((0, 0), (0, 0), (3, 125 - 3 * text_parts[0].shape[2])))
    proj_in, second_map, text_terms, text_parts = lax.optimization_barrier((proj_in, second_map, text_terms, text_parts))

    width = proj_weight.shape[1]
    half = width // 2

    def first_y(hop):
        return dot(pick(proj_in, y + hop, 1).reshape(RING * tokens, feats), proj_weight[:, :half])

    def first_z(hop):
        return dot(pick(proj_in, z + hop, 0).reshape(RING * tokens, feats), proj_weight[:, half:])

    sent = [(along(first_y(hop).astype(bf16), "y", hop), along(first_z(hop).astype(bf16), "z", hop)) for hop in HOPS]
    sent = lax.optimization_barrier(sent)
    over_y = (first_y(0) + sum(part.astype(f32) for part, _ in sent)).reshape(RING, tokens, half)
    over_z = (first_z(0) + sum(part.astype(f32) for _, part in sent)).reshape(RING, tokens, half)
    left = sum_ring(lambda hop: pick(over_y, z + hop, 0), "z")
    right = sum_ring(lambda hop: pick(over_z, y + hop, 0), "y")
    proj_sum = jnp.concatenate([left, right], axis=1)
    proj_hidden = jax.nn.gelu(proj_sum, approximate=False).astype(bf16)

    hidden_ring = gather_ring(proj_hidden, "z", z).reshape(RING * tokens, width)
    def second_part(t):
        t = t % RING
        size = (1, RING, 1) + second_map.shape[3:]
        return lax.dynamic_slice(second_map, (t // 2, 0, t % 2, 0, 0), size).reshape(-1, width)

    second = sum_ring(lambda hop: dot_rows(hidden_ring, second_part(x + hop)), "x")
    piece = second.shape[1]
    bias_piece = lax.dynamic_slice_in_dim(proj2_bias, z * piece, piece)
    second = (second + bias_piece).astype(bf16).reshape(RING, tokens, piece)
    visual = jnp.concatenate(swap_ring(second, "z", z), axis=1)

    first, second = jnp.where(c == 0, y, z), jnp.where(c == 0, z, y)
    columns = qkv_weight.shape[1] // RING
    *sent, seen_sum = seen_terms(x, visual, rms_gain, text_parts, qkv_weight)
    for step in range(RING - 1):
        seen_sum = seen_sum + along(sent[step], "x", to_ring(step)).astype(f32)
    seen_squares = jnp.sum(seen_sum[:, columns : columns + 3], axis=1, keepdims=True)
    text_squares = seen_sum[:, columns + 3 : columns + 9].reshape(tokens, 3, -1).sum(axis=1).reshape(-1, 1)
    seen_qkv = (seen_sum[:, :columns] * lax.rsqrt(seen_squares / D + norm_eps)).astype(bf16)
    seen_ring = jnp.concatenate([seen_qkv] + [along(seen_qkv, "zy", hop) for hop in HOPS], axis=0)
    seen_all = [seen_ring] + [along(seen_ring, "yz", hop) for hop in HOPS]
    seen_all = [part.reshape(-1, BLK, columns) for part in seen_all]

    slots = visual_slot[0]
    local_blocks = text_embed.shape[1] // BLK
    wanted = s * local_blocks + jnp.arange(local_blocks, dtype=jnp.int32)
    matches = slots[None, :] == wanted[:, None]
    owned = jnp.any(matches, axis=1).reshape(RING, -1)
    source = jnp.sum(jnp.where(matches, jnp.arange(slots.shape[0], dtype=jnp.int32)[None, :], 0), axis=1).reshape(RING, -1)
    rows_out = text_embed.shape[1] // RING

    source = pick_groups(source, x).reshape(-1)
    shard_z, shard_y = source // (4 * RING), source // 4 % RING
    order_of = jnp.asarray([0, 2, 1, 3], jnp.int32)
    first_hop = order_of[(second - jnp.where(c == 0, shard_z, shard_y)) % RING]
    second_hop = order_of[(first - jnp.where(c == 0, shard_y, shard_z)) % RING]
    chosen = choose_blocks(second_hop, first_hop * 4 + source % 4, seen_all)
    parts = {0: chosen[0].reshape(rows_out, columns)}
    for hop in HOPS:
        parts[hop] = along(chosen[hop % RING].reshape(rows_out, columns), "x", hop)
    rows_seen = jnp.concatenate(order_ring(parts, x), axis=1)
    text_qkv = (text_sum.astype(f32) * lax.rsqrt(text_squares / D + norm_eps)).astype(bf16)
    row_owned = jnp.repeat(pick(owned, x, 0), BLK)
    return jnp.where(row_owned[:, None], rows_seen, text_qkv)[None]


def solution(mesh):
    return jax.shard_map(
        local,
        mesh=mesh,
        in_specs=(
            P("section", "seq", "tensor"),
            P("section", "seq", "tensor"),
            P("tensor", "seq"),
            P("tensor"),
            P(),
            P(),
            P("seq", "tensor"),
            P("tensor", None, "seq"),
            P("tensor"),
            P("section", "seq", "tensor"),
            P("section", None),
            P("tensor"),
            P("tensor", None),
        ),
        out_specs=P("section", ("seq", "tensor"), None),
        check_vma=False,
    )
```

```python
import jax
import jax.numpy as jnp
import numpy as np
from jax import lax
from jax.experimental import pallas as pl
from jax.experimental.pallas import tpu as pltpu
from jax.sharding import PartitionSpec as P

D = 7168
G = 32
BLK = 16
RING = 4

norm_eps = 1e-05
bf16 = jnp.bfloat16
f32 = jnp.float32
ALL = ("section", "seq", "tensor")


def move(block, target):
    route = []
    for c in range(2):
        for z in range(RING):
            for y in range(RING):
                for x in range(RING):
                    tc, tz, ty, tx = target(c, z, y, x)
                    here = ((c * RING + z) * RING + y) * RING + x
                    there = ((tc % 2 * RING + tz % RING) * RING + ty % RING) * RING + tx % RING
                    route.append((here, there))
    return lax.ppermute(block, ALL, route)


def along(block, axis, hop):
    axes = axis * 2 if len(axis) == 1 else axis

    def target(c, z, y, x):
        return (c, z + hop * (axes[c] == "z"), y + hop * (axes[c] == "y"), x + hop * (axes[c] == "x"))

    return move(block, target)


def pick(array, index, axis):
    return lax.dynamic_index_in_dim(array, index % RING, axis, keepdims=False)


def put(target, block, index, axis):
    return lax.dynamic_update_index_in_dim(target, block, index % RING, axis)


HOPS = (2, 1, -1)


def gather_ring(block, axis, me, stack_axis=0):
    return stack_ring([(hop, along(block, axis, hop)) for hop in HOPS] + [(0, block)], me, stack_axis)


def stack_ring(parts, me, stack_axis=0):
    shape = parts[0][1].shape
    stacked = jnp.zeros(shape[:stack_axis] + (RING,) + shape[stack_axis:], parts[0][1].dtype)
    for hop, part in parts:
        stacked = put(stacked, part, me - hop, stack_axis)
    return stacked


def sum_ring(term, axis, wire=bf16):
    arrived = [along(term(hop).astype(wire), axis, hop) for hop in HOPS]
    total = term(0)
    for part in arrived:
        total = total + part.astype(f32)
    return total


def order_ring(parts, me):
    blocks = [parts[hop] for hop in (0, 1, 2, -1)]
    return [lax.select_n((me - owner) % RING, *blocks) for owner in range(RING)]


def swap_ring(blocks, axis, me):
    parts = {hop: along(pick(blocks, me + hop, 0), axis, hop) for hop in HOPS}
    parts[0] = pick(blocks, me, 0)
    return order_ring(parts, me)


def pick_groups(groups, me):
    return jnp.stack([pick(groups, me + hop, 0) for hop in range(RING)])


def in_parts(value):
    high = lax.reduce_precision(value, 8, 7)
    middle = lax.reduce_precision(value - high, 8, 7)
    return [high, middle, lax.reduce_precision(value - high - middle, 8, 7)]


def after(value, *others):
    return lax.optimization_barrier((value, others))[0]


VMEM = 40 * 2**20


def to_ring(step):
    return RING - 1 - step


def seen_kernel(x_ref, visual_ref, gain_ref, extra_ref, weight_ref, *outs):
    seen = visual_ref[...].astype(f32)
    total = dot((seen * gain_ref[...]).astype(bf16), weight_ref[...])
    wide = total.shape[1]
    columns = outs[0].shape[1] - extra_ref.shape[2]
    part = pl.program_id(1)

    def write(step):
        @pl.when(pl.program_id(0) == step)
        def _():
            outs[step][:, pl.ds(pl.multiple_of(part * wide, 128), wide)] = total.astype(outs[step].dtype)

        @pl.when((pl.program_id(0) == step) & (part == 0))
        def _():
            squares = jnp.sum(seen * seen, axis=1, keepdims=True)
            high = squares.astype(bf16).astype(f32)
            middle = (squares - high).astype(bf16).astype(f32)
            lane = lax.broadcasted_iota(jnp.int32, extra_ref.shape[1:], 1)
            extra = extra_ref[0]
            for place, piece in enumerate((high, middle, squares - high - middle)):
                extra = jnp.where(lane == place, piece, extra)
            outs[step][:, columns:] = extra.astype(outs[step].dtype)

    for step in range(RING):
        write(step)


def seen_terms(x, visual, gain, extra, weight):
    rows, width = visual.shape
    columns = weight.shape[1] // RING
    lanes = extra.shape[2]
    parts = 3
    return pl.pallas_call(
        seen_kernel,
        grid_spec=pltpu.PrefetchScalarGridSpec(
            num_scalar_prefetch=1,
            grid=(RING, parts),
            in_specs=[
                pl.BlockSpec((rows, width), lambda i, j, x: (0, 0)),
                pl.BlockSpec((1, width), lambda i, j, x: (0, 0)),
                pl.BlockSpec((1, rows, lanes), lambda i, j, x: ((x[0] + to_ring(i)) % RING, 0, 0)),
                pl.BlockSpec((width, columns // parts), lambda i, j, x: (0, (x[0] + to_ring(i)) % RING * parts + j)),
            ],
            out_specs=[pl.BlockSpec((rows, columns + lanes), lambda i, j, x: (0, 0))] * RING,
        ),
        out_shape=[jax.ShapeDtypeStruct((rows, columns + lanes), kind) for kind in (bf16, bf16, bf16, f32)],
        compiler_params=pltpu.CompilerParams(vmem_limit_bytes=VMEM),
        cost_estimate=pl.CostEstimate(
            flops=2 * rows * width * columns * RING, bytes_accessed=2 * RING * width * columns, transcendentals=0
        ),
    )(x.reshape(1), visual, gain.reshape(1, width), extra, weight)


def choose_kernel(array_ref, place_ref, *refs):
    arrays, chosen = refs[:RING], refs[RING:]
    for to, out in enumerate(chosen):
        for i in range(out.shape[0]):
            which, place = array_ref[to * out.shape[0] + i], place_ref[to * out.shape[0] + i]
            block = arrays[0][place]
            for other in range(1, RING):
                block = jnp.where(which == other, arrays[other][place], block)
            out[i] = block


def choose_blocks(array, place, arrays):
    count = array.shape[0] // RING
    shape = jax.ShapeDtypeStruct((count,) + arrays[0].shape[1:], arrays[0].dtype)
    return pl.pallas_call(
        choose_kernel,
        in_specs=[pl.BlockSpec(memory_space=pltpu.SMEM)] * 2 + [pl.BlockSpec(memory_space=pltpu.VMEM)] * RING,
        out_specs=[pl.BlockSpec(memory_space=pltpu.VMEM)] * RING,
        out_shape=[shape] * RING,
        compiler_params=pltpu.CompilerParams(vmem_limit_bytes=VMEM),
        cost_estimate=pl.CostEstimate(flops=0, bytes_accessed=2 * RING * arrays[0].size, transcendentals=0),
    )(array, place, *arrays)


def dot(a, b):
    return jnp.dot(a, b, preferred_element_type=f32)


def dot_rows(a, b):
    return lax.dot_general(a, b, (((a.ndim - 1,), (1,)), ((), ())), preferred_element_type=f32)


def patch_order():
    order = np.arange(8 * G).reshape(4, 2, G // 2, 2).transpose(1, 3, 0, 2).reshape(-1)
    return np.eye(8 * G, dtype=np.float32)[order]


def local(
    vit_hidden,
    vit_resid,
    fc2_weight,
    layer_scale,
    norm_gain,
    norm_bias,
    proj_weight,
    proj2_weight,
    proj2_bias,
    text_embed,
    visual_slot,
    rms_gain,
    qkv_weight,
):
    c = lax.axis_index("section")
    s = lax.axis_index("seq")
    x = lax.axis_index("tensor")
    z, y = s // RING, s % RING
    order = jnp.asarray(patch_order(), bf16)
    tokens = vit_hidden.shape[1] // 4
    feats = layer_scale.shape[0]

    hidden = dot(vit_hidden[0].T, order.T).astype(bf16)
    behind = move(hidden, lambda c, z, y, x: (1 - c, z + 1, y, x))
    ahead = move(hidden, lambda c, z, y, x: (1 - c, z - 1, y, x))
    weight = fc2_weight.T
    weight_near = move(weight, lambda c, z, y, x: (c, z, y + 1 - 2 * c, x))
    own = move(hidden, lambda c, z, y, x: (1 - c, z, y, x))
    resid = dot(vit_resid[0].T, order.T).astype(bf16)
    resid = move(resid, lambda c, z, y, x: (1 - c, z, y, x - z))
    far = move(jnp.where(c == 0, behind, ahead), lambda c, z, y, x: (c, z + 1 - 2 * c, y, x))
    weight_far = move(weight_near, lambda c, z, y, x: (c, z, y + 1 - 2 * c, x))
    weight_other = move(weight_near, lambda c, z, y, x: (1 - c, z, y, x))
    resid = move(resid, lambda c, z, y, x: (c, z + x, y, x))
    weight_quarter = jnp.concatenate([weight, weight_near, weight_far, weight_other], axis=0)

    halves = proj2_weight.shape[1] // 2
    second_map = lax.dynamic_slice_in_dim(proj2_weight.transpose(1, 2, 0), c * halves, halves, 0)
    rings = [[16 * core + RING * i + j for core in range(2) for j in range(RING)] for i in range(RING)]
    second_map = lax.all_gather(second_map, ("section", "seq"), axis=0, axis_index_groups=rings)
    second_map = second_map.reshape((2, RING) + second_map.shape[1:])

    resid = move(resid, lambda c, z, y, x: (c, z, y, x - z))
    scale = move(layer_scale, lambda c, z, y, x: (c, x, y, z))[:, None]

    terms = [dot(weight_quarter, rows) for rows in (own, ahead, far, behind)]
    terms, resid = lax.optimization_barrier((terms, resid))
    text = after(text_embed[0], terms).astype(f32)
    text_terms = dot((text * rms_gain).astype(bf16), qkv_weight).astype(bf16)
    text_parts = in_parts(jnp.sum(text * text, axis=1).reshape(RING, tokens, -1))
    text_parts = jnp.pad(jnp.concatenate(text_parts, axis=2), ((0, 0), (0, 0), (3, 125 - 3 * text_parts[0].shape[2])))
    mlp = sum_ring(lambda hop: lax.select_n((-x - hop - z) % RING, *terms), "x")
    mlp, text_terms, text_parts = lax.optimization_barrier((mlp, text_terms, text_parts))
    mlp = mlp.reshape(RING, -1, 4 * tokens)
    mlp = [lax.select_n(jnp.where(c == 0, y - piece, piece - y) % RING, *mlp) for piece in range(RING)]
    layer_out = resid.astype(f32) + scale * jnp.concatenate(mlp, axis=0)
    layer_out = layer_out.astype(bf16).T.reshape(4, tokens, feats)
    widened = layer_out.astype(f32)
    part_mean = jnp.mean(widened, axis=(0, 2))
    part_dev = jnp.sum(jnp.square(widened - part_mean[:, None]), axis=(0, 2))
    part = jnp.stack([part_mean, part_dev])
    parts = jnp.stack([part] + [along(part, "z", hop) for hop in HOPS])
    mean = jnp.mean(parts[:, 0], axis=0)
    dev = jnp.sum(parts[:, 1], axis=0) + 4 * feats * jnp.sum(jnp.square(parts[:, 0] - mean), axis=0)
    inv = lax.rsqrt(dev / (4 * RING * feats) + norm_eps)
    gain = pick(norm_gain.reshape(4, RING, 1, feats), z, 1)
    bias = pick(norm_bias.reshape(4, RING, 1, feats), z, 1)
    proj_in = ((widened - mean[:, None]) * inv[:, None] * gain + bias).astype(bf16)
    proj_in = jnp.stack(swap_ring(proj_in, "z", z))
    proj_in = jnp.stack(swap_ring(proj_in, "y", y))
    arrived = [(hop, along(proj_in, "x", hop)) for hop in HOPS] + [(0, proj_in)]
    proj_in = stack_ring([(-hop, part) for hop, part in arrived], -x)
    proj_in, second_map, text_terms = lax.optimization_barrier((proj_in, second_map, text_terms))
    text_sum = lax.psum_scatter(text_terms, "tensor", scatter_dimension=0, tiled=True)

    width = proj_weight.shape[1]
    half = width // 2

    def first_y(hop):
        return dot(pick(proj_in, y + hop, 1).reshape(RING * tokens, feats), proj_weight[:, :half])

    def first_z(hop):
        return dot(pick(proj_in, z + hop, 0).reshape(RING * tokens, feats), proj_weight[:, half:])

    sent = [(along(first_y(hop).astype(bf16), "y", hop), along(first_z(hop).astype(bf16), "z", hop)) for hop in HOPS]
    sent = lax.optimization_barrier(sent)
    over_y = (first_y(0) + sum(part.astype(f32) for part, _ in sent)).reshape(RING, tokens, half)
    over_z = (first_z(0) + sum(part.astype(f32) for _, part in sent)).reshape(RING, tokens, half)
    left = sum_ring(lambda hop: pick(over_y, z + hop, 0), "z")
    right = sum_ring(lambda hop: pick(over_z, y + hop, 0), "y")
    proj_sum = jnp.concatenate([left, right], axis=1)
    proj_hidden = jax.nn.gelu(proj_sum, approximate=False).astype(bf16)

    hidden_ring = gather_ring(proj_hidden, "z", z).reshape(RING * tokens, width)
    def second_part(t):
        t = t % RING
        size = (1, RING, 1) + second_map.shape[3:]
        return lax.dynamic_slice(second_map, (t // 2, 0, t % 2, 0, 0), size).reshape(-1, width)

    second = sum_ring(lambda hop: dot_rows(hidden_ring, second_part(x + hop)), "x")
    piece = second.shape[1]
    bias_piece = lax.dynamic_slice_in_dim(proj2_bias, z * piece, piece)
    second = (second + bias_piece).astype(bf16).reshape(RING, tokens, piece)
    visual = jnp.concatenate(swap_ring(second, "z", z), axis=1)

    first, second = jnp.where(c == 0, y, z), jnp.where(c == 0, z, y)
    columns = qkv_weight.shape[1] // RING
    *sent, seen_sum = seen_terms(x, visual, rms_gain, text_parts, qkv_weight)
    for step in range(RING - 1):
        seen_sum = seen_sum + along(sent[step], "x", to_ring(step)).astype(f32)
    seen_squares = jnp.sum(seen_sum[:, columns : columns + 3], axis=1, keepdims=True)
    text_squares = seen_sum[:, columns + 3 : columns + 9].reshape(tokens, 3, -1).sum(axis=1).reshape(-1, 1)
    seen_qkv = (seen_sum[:, :columns] * lax.rsqrt(seen_squares / D + norm_eps)).astype(bf16)
    seen_ring = jnp.concatenate([seen_qkv] + [along(seen_qkv, "zy", hop) for hop in HOPS], axis=0)
    seen_all = [seen_ring] + [along(seen_ring, "yz", hop) for hop in HOPS]
    seen_all = [part.reshape(-1, BLK, columns) for part in seen_all]

    slots = visual_slot[0]
    local_blocks = text_embed.shape[1] // BLK
    wanted = s * local_blocks + jnp.arange(local_blocks, dtype=jnp.int32)
    matches = slots[None, :] == wanted[:, None]
    owned = jnp.any(matches, axis=1).reshape(RING, -1)
    source = jnp.sum(jnp.where(matches, jnp.arange(slots.shape[0], dtype=jnp.int32)[None, :], 0), axis=1).reshape(RING, -1)
    rows_out = text_embed.shape[1] // RING

    source = pick_groups(source, x).reshape(-1)
    shard_z, shard_y = source // (4 * RING), source // 4 % RING
    order_of = jnp.asarray([0, 2, 1, 3], jnp.int32)
    first_hop = order_of[(second - jnp.where(c == 0, shard_z, shard_y)) % RING]
    second_hop = order_of[(first - jnp.where(c == 0, shard_y, shard_z)) % RING]
    chosen = choose_blocks(second_hop, first_hop * 4 + source % 4, seen_all)
    parts = {0: chosen[0].reshape(rows_out, columns)}
    for hop in HOPS:
        parts[hop] = along(chosen[hop % RING].reshape(rows_out, columns), "x", hop)
    rows_seen = jnp.concatenate(order_ring(parts, x), axis=1)
    text_qkv = (text_sum.astype(f32) * lax.rsqrt(text_squares / D + norm_eps)).astype(bf16)
    row_owned = jnp.repeat(pick(owned, x, 0), BLK)
    return jnp.where(row_owned[:, None], rows_seen, text_qkv)[None]


def solution(mesh):
    return jax.shard_map(
        local,
        mesh=mesh,
        in_specs=(
            P("section", "seq", "tensor"),
            P("section", "seq", "tensor"),
            P("tensor", "seq"),
            P("tensor"),
            P(),
            P(),
            P("seq", "tensor"),
            P("tensor", None, "seq"),
            P("tensor"),
            P("section", "seq", "tensor"),
            P("section", None),
            P("tensor"),
            P("tensor", None),
        ),
        out_specs=P("section", ("seq", "tensor"), None),
        check_vma=False,
    )
```

```python
import jax
import jax.numpy as jnp
import numpy as np
from jax import lax
from jax.experimental import pallas as pl
from jax.experimental.pallas import tpu as pltpu
from jax.sharding import PartitionSpec as P

D = 7168
G = 32
BLK = 16
RING = 4

norm_eps = 1e-05
bf16 = jnp.bfloat16
f32 = jnp.float32
ALL = ("section", "seq", "tensor")


def move(block, target):
    route = []
    for c in range(2):
        for z in range(RING):
            for y in range(RING):
                for x in range(RING):
                    tc, tz, ty, tx = target(c, z, y, x)
                    here = ((c * RING + z) * RING + y) * RING + x
                    there = ((tc % 2 * RING + tz % RING) * RING + ty % RING) * RING + tx % RING
                    route.append((here, there))
    return lax.ppermute(block, ALL, route)


def along(block, axis, hop):
    axes = axis * 2 if len(axis) == 1 else axis

    def target(c, z, y, x):
        return (c, z + hop * (axes[c] == "z"), y + hop * (axes[c] == "y"), x + hop * (axes[c] == "x"))

    return move(block, target)


def pick(array, index, axis):
    return lax.dynamic_index_in_dim(array, index % RING, axis, keepdims=False)


def put(target, block, index, axis):
    return lax.dynamic_update_index_in_dim(target, block, index % RING, axis)


HOPS = (2, 1, -1)


def gather_ring(block, axis, me, stack_axis=0):
    return stack_ring([(hop, along(block, axis, hop)) for hop in HOPS] + [(0, block)], me, stack_axis)


def stack_ring(parts, me, stack_axis=0):
    shape = parts[0][1].shape
    stacked = jnp.zeros(shape[:stack_axis] + (RING,) + shape[stack_axis:], parts[0][1].dtype)
    for hop, part in parts:
        stacked = put(stacked, part, me - hop, stack_axis)
    return stacked


def sum_ring(term, axis, wire=bf16):
    arrived = [along(term(hop).astype(wire), axis, hop) for hop in HOPS]
    total = term(0)
    for part in arrived:
        total = total + part.astype(f32)
    return total


def order_ring(parts, me):
    blocks = [parts[hop] for hop in (0, 1, 2, -1)]
    return [lax.select_n((me - owner) % RING, *blocks) for owner in range(RING)]


def swap_ring(blocks, axis, me):
    parts = {hop: along(pick(blocks, me + hop, 0), axis, hop) for hop in HOPS}
    parts[0] = pick(blocks, me, 0)
    return order_ring(parts, me)


def pick_groups(groups, me):
    return jnp.stack([pick(groups, me + hop, 0) for hop in range(RING)])


def in_parts(value):
    high = lax.reduce_precision(value, 8, 7)
    middle = lax.reduce_precision(value - high, 8, 7)
    return [high, middle, lax.reduce_precision(value - high - middle, 8, 7)]


def after(value, *others):
    return lax.optimization_barrier((value, others))[0]


VMEM = 40 * 2**20


def to_ring(step):
    return RING - 1 - step


def seen_kernel(x_ref, visual_ref, gain_ref, extra_ref, weight_ref, *refs):
    outs, total_ref, squares_ref = refs[:RING], refs[RING], refs[RING + 1]
    block = pl.program_id(0)

    @pl.when(block == 0)
    def _():
        total_ref[...] = jnp.zeros_like(total_ref)
        squares_ref[...] = jnp.zeros_like(squares_ref)

    seen = visual_ref[...].astype(f32)
    squares_ref[...] += jnp.broadcast_to(jnp.sum(seen * seen, axis=1, keepdims=True), squares_ref.shape)
    total_ref[...] += dot((seen * gain_ref[...]).astype(bf16), weight_ref[...])

    @pl.when(block == pl.num_programs(0) - 1)
    def _():
        squares = squares_ref[...]
        high = squares.astype(bf16).astype(f32)
        middle = (squares - high).astype(bf16).astype(f32)
        lane = lax.broadcasted_iota(jnp.int32, squares.shape, 1)
        columns = total_ref.shape[1] // RING
        for step, out in enumerate(outs):
            to = (x_ref[0] + to_ring(step)) % RING
            extra = extra_ref[to]
            for place, piece in enumerate((high, middle, squares - high - middle)):
                extra = jnp.where(lane == place, piece, extra)
            out[:, :columns] = total_ref[:, pl.ds(pl.multiple_of(to * columns, 128), columns)].astype(out.dtype)
            out[:, columns:] = extra.astype(out.dtype)


def seen_terms(x, visual, gain, extra, weight):
    rows, width = visual.shape
    columns = weight.shape[1] // RING
    lanes = extra.shape[2]
    deep = 256
    return pl.pallas_call(
        seen_kernel,
        grid_spec=pltpu.PrefetchScalarGridSpec(
            num_scalar_prefetch=1,
            grid=(width // deep,),
            in_specs=[
                pl.BlockSpec((rows, deep), lambda i, x: (0, i)),
                pl.BlockSpec((1, deep), lambda i, x: (0, i)),
                pl.BlockSpec(extra.shape, lambda i, x: (0, 0, 0)),
                pl.BlockSpec((deep, RING * columns), lambda i, x: (i, 0)),
            ],
            out_specs=[pl.BlockSpec((rows, columns + lanes), lambda i, x: (0, 0))] * RING,
            scratch_shapes=[pltpu.VMEM((rows, RING * columns), f32), pltpu.VMEM((rows, lanes), f32)],
        ),
        out_shape=[jax.ShapeDtypeStruct((rows, columns + lanes), kind) for kind in (bf16, bf16, bf16, f32)],
        compiler_params=pltpu.CompilerParams(vmem_limit_bytes=VMEM),
        cost_estimate=pl.CostEstimate(
            flops=2 * rows * width * columns * RING, bytes_accessed=2 * RING * width * columns, transcendentals=0
        ),
    )(x.reshape(1), visual, gain.reshape(1, width), extra, weight)


def choose_kernel(array_ref, place_ref, *refs):
    arrays, chosen = refs[:RING], refs[RING:]
    for to, out in enumerate(chosen):
        for i in range(out.shape[0]):
            which, place = array_ref[to * out.shape[0] + i], place_ref[to * out.shape[0] + i]
            block = arrays[0][place]
            for other in range(1, RING):
                block = jnp.where(which == other, arrays[other][place], block)
            out[i] = block


def choose_blocks(array, place, arrays):
    count = array.shape[0] // RING
    shape = jax.ShapeDtypeStruct((count,) + arrays[0].shape[1:], arrays[0].dtype)
    return pl.pallas_call(
        choose_kernel,
        in_specs=[pl.BlockSpec(memory_space=pltpu.SMEM)] * 2 + [pl.BlockSpec(memory_space=pltpu.VMEM)] * RING,
        out_specs=[pl.BlockSpec(memory_space=pltpu.VMEM)] * RING,
        out_shape=[shape] * RING,
        compiler_params=pltpu.CompilerParams(vmem_limit_bytes=VMEM),
        cost_estimate=pl.CostEstimate(flops=0, bytes_accessed=2 * RING * arrays[0].size, transcendentals=0),
    )(array, place, *arrays)


def dot(a, b):
    return jnp.dot(a, b, preferred_element_type=f32)


def dot_rows(a, b):
    return lax.dot_general(a, b, (((a.ndim - 1,), (1,)), ((), ())), preferred_element_type=f32)


def patch_order():
    order = np.arange(8 * G).reshape(4, 2, G // 2, 2).transpose(1, 3, 0, 2).reshape(-1)
    return np.eye(8 * G, dtype=np.float32)[order]


def local(
    vit_hidden,
    vit_resid,
    fc2_weight,
    layer_scale,
    norm_gain,
    norm_bias,
    proj_weight,
    proj2_weight,
    proj2_bias,
    text_embed,
    visual_slot,
    rms_gain,
    qkv_weight,
):
    c = lax.axis_index("section")
    s = lax.axis_index("seq")
    x = lax.axis_index("tensor")
    z, y = s // RING, s % RING
    order = jnp.asarray(patch_order(), bf16)
    tokens = vit_hidden.shape[1] // 4
    feats = layer_scale.shape[0]

    hidden = dot(vit_hidden[0].T, order.T).astype(bf16)
    behind = move(hidden, lambda c, z, y, x: (1 - c, z + 1, y, x))
    ahead = move(hidden, lambda c, z, y, x: (1 - c, z - 1, y, x))
    weight = fc2_weight.T
    weight_near = move(weight, lambda c, z, y, x: (c, z, y + 1 - 2 * c, x))
    own = move(hidden, lambda c, z, y, x: (1 - c, z, y, x))
    resid = dot(vit_resid[0].T, order.T).astype(bf16)
    resid = move(resid, lambda c, z, y, x: (1 - c, z, y, x - z))
    far = move(jnp.where(c == 0, behind, ahead), lambda c, z, y, x: (c, z + 1 - 2 * c, y, x))
    weight_far = move(weight_near, lambda c, z, y, x: (c, z, y + 1 - 2 * c, x))
    weight_other = move(weight_near, lambda c, z, y, x: (1 - c, z, y, x))
    resid = move(resid, lambda c, z, y, x: (c, z + x, y, x))
    weight_quarter = jnp.concatenate([weight, weight_near, weight_far, weight_other], axis=0)

    halves = proj2_weight.shape[1] // 2
    second_map = lax.dynamic_slice_in_dim(proj2_weight.transpose(1, 2, 0), c * halves, halves, 0)
    rings = [[16 * core + RING * i + j for core in range(2) for j in range(RING)] for i in range(RING)]
    second_map = lax.all_gather(second_map, ("section", "seq"), axis=0, axis_index_groups=rings)
    second_map = second_map.reshape((2, RING) + second_map.shape[1:])

    resid = move(resid, lambda c, z, y, x: (c, z, y, x - z))
    scale = move(layer_scale, lambda c, z, y, x: (c, x, y, z))[:, None]

    terms = [dot(weight_quarter, rows) for rows in (own, ahead, far, behind)]
    terms, resid = lax.optimization_barrier((terms, resid))
    mlp = sum_ring(lambda hop: lax.select_n((-x - hop - z) % RING, *terms), "x")
    mlp = mlp.reshape(RING, -1, 4 * tokens)
    mlp = [lax.select_n(jnp.where(c == 0, y - piece, piece - y) % RING, *mlp) for piece in range(RING)]
    layer_out = resid.astype(f32) + scale * jnp.concatenate(mlp, axis=0)
    layer_out = layer_out.astype(bf16).T.reshape(4, tokens, feats)
    widened = layer_out.astype(f32)
    part_mean = jnp.mean(widened, axis=(0, 2))
    part_dev = jnp.sum(jnp.square(widened - part_mean[:, None]), axis=(0, 2))
    part = jnp.stack([part_mean, part_dev])
    parts = jnp.stack([part] + [along(part, "z", hop) for hop in HOPS])
    mean = jnp.mean(parts[:, 0], axis=0)
    dev = jnp.sum(parts[:, 1], axis=0) + 4 * feats * jnp.sum(jnp.square(parts[:, 0] - mean), axis=0)
    inv = lax.rsqrt(dev / (4 * RING * feats) + norm_eps)
    gain = pick(norm_gain.reshape(4, RING, 1, feats), z, 1)
    bias = pick(norm_bias.reshape(4, RING, 1, feats), z, 1)
    proj_in = ((widened - mean[:, None]) * inv[:, None] * gain + bias).astype(bf16)
    proj_in = jnp.stack(swap_ring(proj_in, "z", z))
    proj_in = jnp.stack(swap_ring(proj_in, "y", y))
    text = after(text_embed[0], proj_in).astype(f32)
    arrived = [(hop, along(proj_in, "x", hop)) for hop in HOPS] + [(0, proj_in)]
    proj_in = stack_ring([(-hop, part) for hop, part in arrived], -x)
    text_terms = dot((text * rms_gain).astype(bf16), qkv_weight).astype(bf16)
    text_sum = lax.psum_scatter(text_terms, "tensor", scatter_dimension=0, tiled=True)
    text_parts = in_parts(jnp.sum(text * text, axis=1).reshape(RING, tokens, -1))
    text_parts = jnp.pad(jnp.concatenate(text_parts, axis=2), ((0, 0), (0, 0), (3, 125 - 3 * text_parts[0].shape[2])))
    proj_in, second_map, text_terms, text_parts = lax.optimization_barrier((proj_in, second_map, text_terms, text_parts))

    width = proj_weight.shape[1]
    half = width // 2

    def first_y(hop):
        return dot(pick(proj_in, y + hop, 1).reshape(RING * tokens, feats), proj_weight[:, :half])

    def first_z(hop):
        return dot(pick(proj_in, z + hop, 0).reshape(RING * tokens, feats), proj_weight[:, half:])

    sent = [(along(first_y(hop).astype(bf16), "y", hop), along(first_z(hop).astype(bf16), "z", hop)) for hop in HOPS]
    sent = lax.optimization_barrier(sent)
    over_y = (first_y(0) + sum(part.astype(f32) for part, _ in sent)).reshape(RING, tokens, half)
    over_z = (first_z(0) + sum(part.astype(f32) for _, part in sent)).reshape(RING, tokens, half)
    left = sum_ring(lambda hop: pick(over_y, z + hop, 0), "z")
    right = sum_ring(lambda hop: pick(over_z, y + hop, 0), "y")
    proj_sum = jnp.concatenate([left, right], axis=1)
    proj_hidden = jax.nn.gelu(proj_sum, approximate=False).astype(bf16)

    hidden_ring = gather_ring(proj_hidden, "z", z).reshape(RING * tokens, width)
    def second_part(t):
        t = t % RING
        size = (1, RING, 1) + second_map.shape[3:]
        return lax.dynamic_slice(second_map, (t // 2, 0, t % 2, 0, 0), size).reshape(-1, width)

    second = sum_ring(lambda hop: dot_rows(hidden_ring, second_part(x + hop)), "x")
    piece = second.shape[1]
    bias_piece = lax.dynamic_slice_in_dim(proj2_bias, z * piece, piece)
    second = (second + bias_piece).astype(bf16).reshape(RING, tokens, piece)
    visual = jnp.concatenate(swap_ring(second, "z", z), axis=1)

    first, second = jnp.where(c == 0, y, z), jnp.where(c == 0, z, y)
    columns = qkv_weight.shape[1] // RING
    *sent, seen_sum = seen_terms(x, visual, rms_gain, text_parts, qkv_weight)
    for step in range(RING - 1):
        seen_sum = seen_sum + along(sent[step], "x", to_ring(step)).astype(f32)
    seen_squares = jnp.sum(seen_sum[:, columns : columns + 3], axis=1, keepdims=True)
    text_squares = seen_sum[:, columns + 3 : columns + 9].reshape(tokens, 3, -1).sum(axis=1).reshape(-1, 1)
    seen_qkv = (seen_sum[:, :columns] * lax.rsqrt(seen_squares / D + norm_eps)).astype(bf16)
    seen_ring = jnp.concatenate([seen_qkv] + [along(seen_qkv, "zy", hop) for hop in HOPS], axis=0)
    seen_all = [seen_ring] + [along(seen_ring, "yz", hop) for hop in HOPS]
    seen_all = [part.reshape(-1, BLK, columns) for part in seen_all]

    slots = visual_slot[0]
    local_blocks = text_embed.shape[1] // BLK
    wanted = s * local_blocks + jnp.arange(local_blocks, dtype=jnp.int32)
    matches = slots[None, :] == wanted[:, None]
    owned = jnp.any(matches, axis=1).reshape(RING, -1)
    source = jnp.sum(jnp.where(matches, jnp.arange(slots.shape[0], dtype=jnp.int32)[None, :], 0), axis=1).reshape(RING, -1)
    rows_out = text_embed.shape[1] // RING

    source = pick_groups(source, x).reshape(-1)
    shard_z, shard_y = source // (4 * RING), source // 4 % RING
    order_of = jnp.asarray([0, 2, 1, 3], jnp.int32)
    first_hop = order_of[(second - jnp.where(c == 0, shard_z, shard_y)) % RING]
    second_hop = order_of[(first - jnp.where(c == 0, shard_y, shard_z)) % RING]
    chosen = choose_blocks(second_hop, first_hop * 4 + source % 4, seen_all)
    parts = {0: chosen[0].reshape(rows_out, columns)}
    for hop in HOPS:
        parts[hop] = along(chosen[hop % RING].reshape(rows_out, columns), "x", hop)
    rows_seen = jnp.concatenate(order_ring(parts, x), axis=1)
    text_qkv = (text_sum.astype(f32) * lax.rsqrt(text_squares / D + norm_eps)).astype(bf16)
    row_owned = jnp.repeat(pick(owned, x, 0), BLK)
    return jnp.where(row_owned[:, None], rows_seen, text_qkv)[None]


def solution(mesh):
    return jax.shard_map(
        local,
        mesh=mesh,
        in_specs=(
            P("section", "seq", "tensor"),
            P("section", "seq", "tensor"),
            P("tensor", "seq"),
            P("tensor"),
            P(),
            P(),
            P("seq", "tensor"),
            P("tensor", None, "seq"),
            P("tensor"),
            P("section", "seq", "tensor"),
            P("section", None),
            P("tensor"),
            P("tensor", None),
        ),
        out_specs=P("section", ("seq", "tensor"), None),
        check_vma=False,
    )
```
